32 devices in a mesh: seq: 8 (over z, core), dp: 4 (over y, x).
Axes of the slice: x: 2, y: 2, z: 4, core: 2. Of those that a mesh axis runs over, the one named last changes fastest.
Arguments:
- raw_query: bfloat16 [4, 2048, 2048], P('dp', 'seq'), may hold values from -4 to 4
- raw_key: bfloat16 [4, 2048, 2048], P('dp', 'seq'), may hold values from -4 to 4
- raw_value: bfloat16 [4, 2048, 2048], P('dp', 'seq'), may hold values from -6 to 6
- query_gain: float32 [128], replicated, may hold values from 0.5 to 8
- key_gain: float32 [128], replicated, may hold values from 0.5 to 8
- lengths: int32 [16], replicated, may hold values from 1 to 2048, 8192 in all
- clip_grids: int32 [16, 2], replicated, may hold values from 4 to 23
Outputs:
- attended: bfloat16 [4, 2048, 2048], P('dp', 'seq')
The draws below stay inside these ranges and needn't reach their ends.
All inputs are finite; a program needn't handle non-finite values.
Results may differ from the reference program's by a relative error of at most 0.0017.
The reference program's roundings to bfloat16 on the way count: a program that leaves them out, or rounds other values in their place, can miss the bound.
Values may be sent and summed in bfloat16 or wider, within the bound.
A program may use at most 64 MiB of HBM per device.

```python
import math
import jax
import jax.numpy as jnp
import numpy as np
from jax import lax

HEADS = 16
HEAD_DIM = 128
PACK = 2048
PACKS = 4
TOKENS = 8192
WIDTH = 2048
MOST = 2048
CLIPS = 16


def query_key_pair(key):
    base_key = jax.random.fold_in(key, 17)
    first_key, second_key = jax.random.split(base_key, 2)
    shape = (PACKS, PACK, WIDTH)
    key_part = jax.random.truncated_normal(first_key, -4.0, 4.0, shape, jnp.float32)
    query_part = jax.random.truncated_normal(second_key, -4.0, 4.0, shape, jnp.float32)
    return (query_part, key_part)


def draw_raw_query(key, part):
    return query_key_pair(key)[0].astype(jnp.bfloat16)


def draw_raw_key(key, part):
    return query_key_pair(key)[1].astype(jnp.bfloat16)


def gain_draw(key, salt):
    sub_key = jax.random.fold_in(key, salt)
    low_end, high_end = (0.5, 2.0)
    return jnp.exp(jax.random.uniform(sub_key, (HEAD_DIM,), jnp.float32, math.log(low_end), math.log(high_end)))


def draw_query_gain(key, part):
    return gain_draw(key, 31)


def draw_key_gain(key, part):
    return gain_draw(key, 43)


def touch_ends(values, rng, low, high):
    shape = values.shape
    spot = [jax.random.randint(jax.random.fold_in(rng, axis), (), 0, shape[axis]) for axis in range(len(shape))]
    values = values.at[tuple(spot)].set(low)
    longest = shape.index(max(shape))
    spot[longest] = (spot[longest] + 1) % shape[longest]
    return values.at[tuple(spot)].set(high)


def steps_of(rng, extent, cuts, low, high):
    def one(position, parts):
        steps = jax.random.uniform(jax.random.fold_in(jax.random.fold_in(rng, 6), position), (parts,), jnp.float32, low / len(cuts), high / len(cuts))
        return jnp.repeat(jnp.exp(steps), extent[position] // parts).reshape((-1,) + (1,) * (len(extent) - position - 1))

    gain = one(*cuts[0])
    for cut in cuts[1:]:
        gain = gain * one(*cut)
    return gain


def length_profile(count, total, most, slope):
    weights = [(1 << 20) // math.isqrt(grade ** slope) + 1 for grade in range(2, count + 1)]
    spare, holding = total - most - (count - 1), [1] * (count - 1)
    while spare > 0:
        free = [i for i in range(count - 1) if holding[i] < most]
        pool, budget = sum([weights[i] for i in free]), spare
        for i in free:
            addition = min(most - holding[i], max(1, budget * weights[i] // pool), spare)
            holding[i] = holding[i] + addition
            spare = spare - addition
    return np.array([most] + holding)


def uneven_parts(key, number_of, total, bound, lean):
    if number_of == 2:
        one = jax.random.randint(key, (), max(1, total - bound), min(bound, total - 1) + 1)
        return jnp.stack([one, total - one])
    sizes = jnp.asarray(length_profile(number_of, total, bound, lean), jnp.int32)
    couples = (number_of - 1) // 2
    giver, sink = sizes[1:1 + 2 * couples:2], sizes[2:2 + 2 * couples:2]
    room = jnp.minimum(giver - 1, bound - sink)
    passed = jax.random.randint(jax.random.fold_in(key, 1), (couples,), 0, 1 << 20) % (room + 1)
    sizes = sizes.at[1:1 + 2 * couples:2].set(giver - passed).at[2:2 + 2 * couples:2].set(sink + passed)
    return sizes[jax.random.permutation(jax.random.fold_in(key, 2), number_of)]


def normal_values(key, dims, spread, reach, cuts=(), kind=jnp.bfloat16):
    gain = steps_of(key, dims, cuts, -0.22, 0.18) if cuts else 1.0
    array = jax.random.normal(key, dims, jnp.float32) * spread * gain
    return jnp.minimum(jnp.maximum(array, -reach), reach).astype(kind)


def setup_inputs(seed: int = 0) -> dict:
    arg_keys = jax.random.split(jax.random.key(seed), 8)
    raw_query = draw_raw_query(jax.random.fold_in(arg_keys[7], 71), 0)
    raw_key = draw_raw_key(jax.random.fold_in(arg_keys[7], 71), 0)
    raw_value = normal_values(arg_keys[2], (PACKS, PACK, WIDTH), 1.0, 6.0, ((0, 4), (1, 8)))
    query_gain = draw_query_gain(jax.random.fold_in(arg_keys[7], 71), 0)
    key_gain = draw_key_gain(jax.random.fold_in(arg_keys[7], 71), 0)
    lengths = uneven_parts(arg_keys[5], CLIPS, TOKENS, MOST, 2).astype(jnp.int32)
    clip_grids = touch_ends(jax.random.randint(arg_keys[6], (CLIPS, 2), 4, 24), jax.random.fold_in(arg_keys[6], 1), 4, 23).astype(jnp.int32)
    return dict(raw_query=raw_query, raw_key=raw_key, raw_value=raw_value, query_gain=query_gain, key_gain=key_gain, lengths=lengths, clip_grids=clip_grids)


NORM_EPS = 1e-06
ROPE_THETA = 256.0
SCORE_SCALE = 1.0 / math.sqrt(128.0)
MASK_FLOOR = -1e+30

def angle_rates():
    pair_num = jnp.arange(128, dtype=jnp.int32) // 2
    pair_real = pair_num.astype(jnp.float32)
    time_rate = jnp.where(pair_num < 8, ROPE_THETA ** (-2.0 * pair_real / 16.0), 0.0)
    height_rate = jnp.where((pair_num >= 8) & (pair_num < 36), ROPE_THETA ** (-2.0 * (pair_real - 8.0) / 56.0), 0.0)
    width_rate = jnp.where(pair_num >= 36, ROPE_THETA ** (-2.0 * (pair_real - 36.0) / 56.0), 0.0)
    return (time_rate, height_rate, width_rate)

def clip_lookup(global_row, lengths):
    clip_ends = jnp.cumsum(lengths).astype(jnp.int32)
    clip_starts = (clip_ends - lengths).astype(jnp.int32)
    clip_id = lax.optimization_barrier(jnp.sum((global_row[:, None] >= clip_ends[None, :]).astype(jnp.int32), axis=1)).astype(jnp.int32)
    one_hot = (clip_id[:, None] == jnp.arange(lengths.shape[0], dtype=jnp.int32)[None, :]).astype(jnp.int32)
    clip_start = lax.optimization_barrier(jnp.sum(one_hot * clip_starts[None, :], axis=1)).astype(jnp.int32)
    clip_end = lax.optimization_barrier(jnp.sum(one_hot * clip_ends[None, :], axis=1)).astype(jnp.int32)
    return (clip_id, clip_start, clip_end, one_hot)

def rope_tables(lookup, global_row, clip_grids):
    clip_start = lookup[1]
    one_hot = lookup[3]
    height = lax.optimization_barrier(jnp.sum(one_hot * clip_grids[None, :, 0], axis=1)).astype(jnp.int32)
    breadth = lax.optimization_barrier(jnp.sum(one_hot * clip_grids[None, :, 1], axis=1)).astype(jnp.int32)
    offset = global_row - clip_start
    frame_pos = offset // (height * breadth)
    row_pos = offset // breadth % height
    col_pos = offset % breadth
    time_rate, height_rate, width_rate = angle_rates()
    angles = frame_pos.astype(jnp.float32)[:, None] * time_rate[None, :] + row_pos.astype(jnp.float32)[:, None] * height_rate[None, :] + col_pos.astype(jnp.float32)[:, None] * width_rate[None, :]
    return (jnp.cos(angles)[:, None, :], jnp.sin(angles)[:, None, :])

def prepare(raw_rows, gain_vec, cosine_part, sine_part):
    as_float = raw_rows.astype(jnp.float32)
    scaled = as_float * lax.rsqrt(lax.optimization_barrier(jnp.mean(as_float * as_float, axis=-1, keepdims=True)) + NORM_EPS) * gain_vec
    pair_view = scaled.reshape(scaled.shape[:-1] + (64, 2))
    swapped = jnp.stack([-pair_view[..., 1], pair_view[..., 0]], axis=-1).reshape(scaled.shape)
    return (scaled * cosine_part + swapped * sine_part).astype(jnp.bfloat16)

def attend(queries, query_clip, key_rows, value_rows, key_clip, low_tile, high_tile, tile_rows):
    row_count = queries.shape[0]
    head_count = queries.shape[1]
    query_wide = queries.astype(jnp.float32)
    start_carry = (jnp.full((row_count, head_count), MASK_FLOOR, jnp.float32), jnp.zeros((row_count, head_count), jnp.float32), jnp.zeros((row_count, head_count, queries.shape[2]), jnp.float32))

    def visit_tile(tile_num, tile_carry):
        row_max, row_sum, weighted = tile_carry
        key_start = tile_num * tile_rows
        key_tile = lax.dynamic_slice_in_dim(key_rows, key_start, tile_rows, 0).astype(jnp.float32)
        value_tile = lax.dynamic_slice_in_dim(value_rows, key_start, tile_rows, 0)
        clip_tile = lax.dynamic_slice_in_dim(key_clip, key_start, tile_rows, 0)
        scores = jnp.einsum('qhd,khd->qhk', query_wide, key_tile) * SCORE_SCALE
        same_clip = (query_clip[:, None] == clip_tile[None, :])[:, None, :]
        new_max = jnp.maximum(row_max, lax.optimization_barrier(jnp.max(jnp.where(same_clip, scores, MASK_FLOOR), axis=2)))
        weights = jnp.where(same_clip, jnp.exp(scores - new_max[..., None]), 0.0)
        shrink = jnp.exp(row_max - new_max)
        row_sum = row_sum * shrink + lax.optimization_barrier(jnp.sum(weights, axis=2))
        rounded = weights.astype(jnp.bfloat16).astype(jnp.float32)
        weighted = weighted * shrink[..., None] + jnp.einsum('qhk,khd->qhd', rounded, value_tile.astype(jnp.float32))
        return (new_max, row_sum, weighted)
    row_max, row_sum, weighted = lax.fori_loop(low_tile, high_tile, visit_tile, start_carry)
    return (row_sum, weighted)

def attend_rows(queries, query_clip, low_tiles, high_tiles, key_rows, value_rows, key_clip, tile_rows):
    tile_count = queries.shape[0] // tile_rows

    def one_tile(tile_num):
        query_tile = lax.dynamic_slice_in_dim(queries, tile_num * tile_rows, tile_rows, 0)
        clip_tile = lax.dynamic_slice_in_dim(query_clip, tile_num * tile_rows, tile_rows, 0)
        low_tile = lax.dynamic_index_in_dim(low_tiles, tile_num, keepdims=False)
        high_tile = lax.dynamic_index_in_dim(high_tiles, tile_num, keepdims=False)
        row_sum, weighted = attend(query_tile, clip_tile, key_rows, value_rows, key_clip, low_tile, high_tile, tile_rows)
        return (weighted / row_sum[..., None]).astype(jnp.bfloat16)
    tiles_out = lax.map(one_tile, jnp.arange(tile_count, dtype=jnp.int32))
    return tiles_out.reshape(queries.shape)

def reference(raw_query, raw_key, raw_value, query_gain, key_gain, lengths, clip_grids):
    global_row = jnp.arange(TOKENS, dtype=jnp.int32)
    lookup = clip_lookup(global_row, lengths)
    cosine_part, sine_part = rope_tables(lookup, global_row, clip_grids)
    queries = prepare(raw_query.reshape(TOKENS, HEADS, HEAD_DIM), query_gain, cosine_part, sine_part)
    key_rows = prepare(raw_key.reshape(TOKENS, HEADS, HEAD_DIM), key_gain, cosine_part, sine_part)
    value_rows = raw_value.reshape(TOKENS, HEADS, HEAD_DIM)
    tile_rows = math.gcd(PACK, 512)
    clip_id, clip_start, clip_end = (lookup[0], lookup[1], lookup[2])
    low_tiles = (clip_start.reshape(-1, tile_rows)[:, 0] // tile_rows).astype(jnp.int32)
    high_tiles = ((clip_end.reshape(-1, tile_rows)[:, -1] + tile_rows - 1) // tile_rows).astype(jnp.int32)
    attended = attend_rows(queries, clip_id, low_tiles, high_tiles, key_rows, value_rows, clip_id, tile_rows)
    return attended.reshape(PACKS, PACK, WIDTH)
```

```python
import functools
import math

import jax
import jax.numpy as jnp
import numpy as np
from jax import lax
from jax.experimental import pallas as pl
from jax.experimental.pallas import tpu as pltpu
from jax.sharding import PartitionSpec as P

NORM_EPS = 1e-06
ROPE_THETA = 256.0
SCORE_SCALE = 1.0 / math.sqrt(128.0)
MASK_FLOOR = -1e30
HEAD = 128
VMEM_LIMIT = 48 * 1024 * 1024


def angle_rates():
    pair = np.arange(HEAD) // 2
    rates = np.zeros((8, HEAD), np.float64)
    rates[0] = np.where(pair < 8, ROPE_THETA ** (-2.0 * pair / 16.0), 0.0)
    rates[1] = np.where((pair >= 8) & (pair < 36), ROPE_THETA ** (-2.0 * (pair - 8.0) / 56.0), 0.0)
    rates[2] = np.where(pair >= 36, ROPE_THETA ** (-2.0 * (pair - 36.0) / 56.0), 0.0)
    return jnp.asarray(rates, jnp.float32)


def swap_matrix():
    m = np.zeros((HEAD, HEAD), np.float32)
    for k in range(HEAD // 2):
        m[2 * k + 1, 2 * k] = -1.0
        m[2 * k, 2 * k + 1] = 1.0
    return jnp.asarray(m, jnp.bfloat16)


def swap_abs(gain):
    return gain.reshape(-1, 2)[:, ::-1].reshape(-1)


def clip_range(lengths_ref, first_row, last_row):
    def step(c, carry):
        cum, c_lo, s_lo, c_hi, e_hi = carry
        end = cum + lengths_ref[c]
        in_lo = (first_row >= cum) & (first_row < end)
        in_hi = (last_row >= cum) & (last_row < end)
        return (
            end,
            jnp.where(in_lo, c, c_lo),
            jnp.where(in_lo, cum, s_lo),
            jnp.where(in_hi, c, c_hi),
            jnp.where(in_hi, end, e_hi),
        )

    zero = jnp.int32(0)
    out = lax.fori_loop(0, lengths_ref.shape[0], step, (zero, zero, zero, zero, zero))
    return out[1:]


def prep_kernel(
    lengths_ref, grids_ref, q_ref, k_ref, v_ref, gains_ref, rates_ref, swap_ref,
    qo_ref, ko_ref, vo_ref,
):
    rows, width = q_ref.shape
    parts, _, cols = qo_ref.shape
    seq_count = lax.axis_size("seq")
    first = (lax.axis_index("dp") * seq_count + lax.axis_index("seq")) * rows
    c_lo, s_lo, c_hi, _ = clip_range(lengths_ref, first, first + rows - 1)
    token = first + lax.broadcasted_iota(jnp.int32, (rows, HEAD), 0)

    def pick(c, carry):
        cum, start, high, wide = carry
        inside = token >= cum
        start = jnp.where(inside, cum, start)
        high = jnp.where(inside, grids_ref[c, 0].astype(jnp.float32), high)
        wide = jnp.where(inside, grids_ref[c, 1].astype(jnp.float32), wide)
        return (cum + lengths_ref[c], start, high, wide)

    ones = jnp.ones((rows, HEAD), jnp.float32)
    _, start, high, wide = lax.fori_loop(
        c_lo, c_hi + 1, pick, (s_lo, jnp.zeros((rows, HEAD), jnp.int32), ones, ones)
    )
    offset = (token - start).astype(jnp.float32)
    line = jnp.floor((offset + 0.5) / wide)
    col = offset - line * wide
    frame = jnp.floor((line + 0.5) / high)
    row = line - frame * high
    angles = frame * rates_ref[0:1] + row * rates_ref[1:2] + col * rates_ref[2:3]
    cosine = jnp.cos(angles)
    sine = jnp.sin(angles)
    swap = swap_ref[...]
    for x_ref, o_ref, g in ((k_ref, ko_ref, 2), (q_ref, qo_ref, 0)):
        cos_g = cosine
        gain, gain_sw = gains_ref[g : g + 1], gains_ref[g + 1 : g + 2]
        for h in range(width // HEAD):
            raw = x_ref[:, h * HEAD : (h + 1) * HEAD]
            x = raw.astype(jnp.float32)
            sw = jnp.dot(raw, swap, preferred_element_type=jnp.float32)
            inv = lax.rsqrt(jnp.mean(x * x, axis=-1, keepdims=True) + NORM_EPS)
            out = (x * inv * gain) * cos_g + (sw * inv * gain_sw) * sine
            p, o = (h * HEAD) // cols, (h * HEAD) % cols
            o_ref[p, :, o : o + HEAD] = out.astype(jnp.bfloat16)
    for p in range(parts):
        vo_ref[p] = v_ref[:, p * cols : (p + 1) * cols]


def attend_kernel(
    lengths_ref, q_ref, kl_ref, ko_ref, kh_ref, vl_ref, vo_ref, vh_ref, o_ref, *, bq, bk
):
    pack, cols = q_ref.shape
    heads = cols // HEAD
    tiles = pack // bk
    pack_base = lax.axis_index("dp") * pack
    base = pack_base - pack

    @pl.loop(0, pack // bq)
    def _(qt):
        r0 = pl.multiple_of(qt * bq, bq)
        first = pack_base + r0
        c_lo, s_lo, c_hi, e_hi = clip_range(lengths_ref, first, first + bq - 1)
        token = first + lax.broadcasted_iota(jnp.int32, (bq, HEAD), 0)

        def pick(c, carry):
            cum, start, end = carry
            inside = token >= cum
            nxt = cum + lengths_ref[c]
            return (nxt, jnp.where(inside, cum, start), jnp.where(inside, nxt, end))

        zeros = jnp.zeros((bq, HEAD), jnp.int32)
        _, start, end = lax.fori_loop(c_lo, c_hi + 1, pick, (s_lo, zeros, zeros))
        start = start[:, :1] - base
        end = end[:, :1] - base
        low = (s_lo - base) // bk
        high = (e_hi - base + bk - 1) // bk
        qs = [q_ref[pl.ds(r0, bq), h * HEAD : (h + 1) * HEAD] for h in range(heads)]

        def segment(k_ref, v_ref, seg, carry):
            def visit(t, carry):
                k0 = pl.multiple_of((t - seg * tiles) * bk, bk)
                idx = t * bk + lax.broadcasted_iota(jnp.int32, (bq, bk), 1)
                same = (idx >= start) & (idx < end)
                out = []
                for h in range(heads):
                    m, l, acc = carry[h]
                    hs = slice(h * HEAD, (h + 1) * HEAD)
                    k = k_ref[pl.ds(k0, bk), hs]
                    v = v_ref[pl.ds(k0, bk), hs]
                    s = lax.dot_general(
                        qs[h], k, (((1,), (1,)), ((), ())), preferred_element_type=jnp.float32
                    ) * SCORE_SCALE
                    s = jnp.where(same, s, MASK_FLOOR)
                    new_m = jnp.maximum(m, jnp.max(s, axis=1, keepdims=True))
                    w = jnp.exp(s - new_m)
                    shrink = jnp.exp(m - new_m)
                    l = l * shrink + jnp.sum(w, axis=1, keepdims=True)
                    acc = acc * shrink + jnp.dot(
                        w.astype(jnp.bfloat16), v, preferred_element_type=jnp.float32
                    )
                    out.append((new_m, l, acc))
                return tuple(out)

            return lax.fori_loop(
                jnp.maximum(low, seg * tiles), jnp.minimum(high, (seg + 1) * tiles), visit, carry
            )

        carry = tuple(
            (
                jnp.full((bq, 1), MASK_FLOOR, jnp.float32),
                jnp.zeros((bq, 1), jnp.float32),
                jnp.zeros((bq, HEAD), jnp.float32),
            )
            for _ in range(heads)
        )
        carry = segment(kl_ref, vl_ref, 0, carry)
        carry = segment(ko_ref, vo_ref, 1, carry)
        carry = segment(kh_ref, vh_ref, 2, carry)
        for h in range(heads):
            _, l, acc = carry[h]
            o_ref[pl.ds(r0, bq), h * HEAD : (h + 1) * HEAD] = (acc / l).astype(jnp.bfloat16)


def in_vmem():
    return pl.BlockSpec(memory_space=pltpu.VMEM)


def in_smem():
    return pl.BlockSpec(memory_space=pltpu.SMEM)


def shards(raw_query, raw_key, raw_value, query_gain, key_gain, lengths, clip_grids):
    _, rows, width = raw_query.shape
    seq = lax.axis_size("seq")
    dp = lax.axis_size("dp")
    pack = rows * seq
    cols = width // seq
    bk = math.gcd(pack, 512)
    bq = math.gcd(pack, 256)
    gains = jnp.stack([query_gain, swap_abs(query_gain), key_gain, swap_abs(key_gain)] * 2)
    part = jax.ShapeDtypeStruct((seq, rows, cols), jnp.bfloat16)
    q, k, v = pl.pallas_call(
        prep_kernel,
        out_shape=(part, part, part),
        in_specs=[in_smem(), in_smem()] + [in_vmem()] * 6,
        out_specs=(in_vmem(),) * 3,
        compiler_params=pltpu.CompilerParams(vmem_limit_bytes=VMEM_LIMIT),
        name="prep",
    )(
        lengths, clip_grids, raw_query[0], raw_key[0], raw_value[0],
        gains, angle_rates(), swap_matrix(),
    )

    def swap_all(x):
        return lax.all_to_all(x, "seq", split_axis=0, concat_axis=0, tiled=True)

    k = swap_all(k).reshape(pack, cols)
    v = swap_all(v).reshape(pack, cols)
    up = [(i, i + 1) for i in range(dp - 1)]
    down = [(i + 1, i) for i in range(dp - 1)]
    k_low, v_low = lax.ppermute(k, "dp", up), lax.ppermute(v, "dp", up)
    k_high, v_high = lax.ppermute(k, "dp", down), lax.ppermute(v, "dp", down)
    q = swap_all(q).reshape(pack, cols)
    out = pl.pallas_call(
        functools.partial(attend_kernel, bq=bq, bk=bk),
        out_shape=jax.ShapeDtypeStruct((pack, cols), jnp.bfloat16),
        in_specs=[in_smem()] + [in_vmem()] * 7,
        out_specs=in_vmem(),
        compiler_params=pltpu.CompilerParams(vmem_limit_bytes=VMEM_LIMIT),
        name="attend",
    )(lengths, q, k_low, k, k_high, v_low, v, v_high)
    out = swap_all(out.reshape(seq, rows, cols))
    return out.transpose(1, 0, 2).reshape(1, rows, width)


def solution(mesh):
    rows = P("dp", "seq", None)
    return jax.shard_map(
        shards,
        mesh=mesh,
        in_specs=(rows, rows, rows, P(), P(), P(), P()),
        out_specs=rows,
        check_vma=False,
    )
```

```python
import functools
import math

import jax
import jax.numpy as jnp
import numpy as np
from jax import lax
from jax.experimental import pallas as pl
from jax.experimental.pallas import tpu as pltpu
from jax.sharding import PartitionSpec as P

NORM_EPS = 1e-06
ROPE_THETA = 256.0
SCORE_SCALE = 1.0 / math.sqrt(128.0)
MASK_FLOOR = -1e30
HEAD = 128
VMEM_LIMIT = 48 * 1024 * 1024


def angle_rates():
    pair = np.arange(HEAD) // 2
    rates = np.zeros((8, HEAD), np.float64)
    rates[0] = np.where(pair < 8, ROPE_THETA ** (-2.0 * pair / 16.0), 0.0)
    rates[1] = np.where((pair >= 8) & (pair < 36), ROPE_THETA ** (-2.0 * (pair - 8.0) / 56.0), 0.0)
    rates[2] = np.where(pair >= 36, ROPE_THETA ** (-2.0 * (pair - 36.0) / 56.0), 0.0)
    return jnp.asarray(rates, jnp.float32)


def swap_matrix():
    m = np.zeros((HEAD, HEAD), np.float32)
    for k in range(HEAD // 2):
        m[2 * k + 1, 2 * k] = -1.0
        m[2 * k, 2 * k + 1] = 1.0
    return jnp.asarray(m, jnp.bfloat16)


def swap_abs(gain):
    return gain.reshape(-1, 2)[:, ::-1].reshape(-1)


def clip_range(lengths_ref, first_row, last_row):
    def step(c, carry):
        cum, c_lo, s_lo, c_hi, e_hi = carry
        end = cum + lengths_ref[c]
        in_lo = (first_row >= cum) & (first_row < end)
        in_hi = (last_row >= cum) & (last_row < end)
        return (
            end,
            jnp.where(in_lo, c, c_lo),
            jnp.where(in_lo, cum, s_lo),
            jnp.where(in_hi, c, c_hi),
            jnp.where(in_hi, end, e_hi),
        )

    zero = jnp.int32(0)
    out = lax.fori_loop(0, lengths_ref.shape[0], step, (zero, zero, zero, zero, zero))
    return out[1:]


def prep_kernel(
    lengths_ref, grids_ref, q_ref, k_ref, v_ref, gains_ref, rates_ref, swap_ref,
    qo_ref, ko_ref, vo_ref,
):
    rows, width = q_ref.shape
    parts, _, cols = qo_ref.shape
    seq_count = lax.axis_size("seq")
    first = (lax.axis_index("dp") * seq_count + lax.axis_index("seq")) * rows
    c_lo, s_lo, c_hi, _ = clip_range(lengths_ref, first, first + rows - 1)
    token = first + lax.broadcasted_iota(jnp.int32, (rows, HEAD), 0)

    def pick(c, carry):
        cum, start, high, wide = carry
        inside = token >= cum
        start = jnp.where(inside, cum, start)
        high = jnp.where(inside, grids_ref[c, 0].astype(jnp.float32), high)
        wide = jnp.where(inside, grids_ref[c, 1].astype(jnp.float32), wide)
        return (cum + lengths_ref[c], start, high, wide)

    ones = jnp.ones((rows, HEAD), jnp.float32)
    _, start, high, wide = lax.fori_loop(
        c_lo, c_hi + 1, pick, (s_lo, jnp.zeros((rows, HEAD), jnp.int32), ones, ones)
    )
    offset = (token - start).astype(jnp.float32)
    line = jnp.floor((offset + 0.5) / wide)
    col = offset - line * wide
    frame = jnp.floor((line + 0.5) / high)
    row = line - frame * high
    angles = frame * rates_ref[0:1] + row * rates_ref[1:2] + col * rates_ref[2:3]
    cosine = jnp.cos(angles)
    sine = jnp.sin(angles)
    swap = swap_ref[...]
    for x_ref, o_ref, g in ((k_ref, ko_ref, 2), (q_ref, qo_ref, 0)):
        cos_g = cosine
        gain, gain_sw = gains_ref[g : g + 1], gains_ref[g + 1 : g + 2]
        for h in range(width // HEAD):
            raw = x_ref[:, h * HEAD : (h + 1) * HEAD]
            x = raw.astype(jnp.float32)
            sw = jnp.dot(raw, swap, preferred_element_type=jnp.float32)
            inv = lax.rsqrt(jnp.mean(x * x, axis=-1, keepdims=True) + NORM_EPS)
            out = (x * inv * gain) * cos_g + (sw * inv * gain_sw) * sine
            p, o = (h * HEAD) // cols, (h * HEAD) % cols
            o_ref[p, :, o : o + HEAD] = out.astype(jnp.bfloat16)
    for p in range(parts):
        vo_ref[p] = v_ref[:, p * cols : (p + 1) * cols]


def remote(src, dst, send_sem, recv_sem, where):
    return pltpu.make_async_remote_copy(
        src_ref=src, dst_ref=dst, send_sem=send_sem, recv_sem=recv_sem,
        device_id=where, device_id_type=pl.DeviceIdType.MESH,
    )


def exchange_kernel(
    q_in, k_in, v_in, q_out, k_out, v_out, k_low, v_low, k_high, v_high,
    own_sem, send_sem, recv_sem, up_send, up_recv, down_send, down_recv,
):
    seq = lax.axis_size("seq")
    dp = lax.axis_size("dp")
    me = lax.axis_index("seq")
    pack = lax.axis_index("dp")
    has_low = pack > 0
    has_high = pack < dp - 1
    barrier = pltpu.get_barrier_semaphore()

    def signal(where):
        pl.semaphore_signal(barrier, inc=1, device_id=where, device_id_type=pl.DeviceIdType.MESH)

    @pl.loop(1, seq)
    def _(i):
        signal({"seq": lax.rem(me + i, seq)})

    signal({"dp": lax.rem(pack + 1, dp)})
    signal({"dp": lax.rem(pack + dp - 1, dp)})
    pl.semaphore_wait(barrier, seq + 1)

    ins = (k_in, v_in, q_in)
    outs = (k_out, v_out, q_out)
    lows = (k_low, v_low)
    highs = (k_high, v_high)

    def send(a, i):
        to = lax.rem(me + i, seq)
        return remote(
            ins[a].at[to], outs[a].at[me], send_sem.at[a, to], recv_sem.at[a, me], {"seq": to}
        )

    def arrival(a, src):
        return remote(
            ins[a].at[src], outs[a].at[src], send_sem.at[a, src], recv_sem.at[a, src],
            {"seq": src},
        )

    def go_up(a, src_ref, src):
        return remote(
            src_ref, lows[a].at[src], up_send.at[a, src], up_recv.at[a, src], {"dp": pack + 1}
        )

    def go_down(a, src_ref, src):
        return remote(
            src_ref, highs[a].at[src], down_send.at[a, src], down_recv.at[a, src],
            {"dp": pack - 1},
        )

    def forward(a, src_ref, src):
        @pl.when(has_high)
        def _():
            go_up(a, src_ref, src).start()

        @pl.when(has_low)
        def _():
            go_down(a, src_ref, src).start()

    @pl.loop(1, seq)
    def _(i):
        send(0, i).start()
        send(1, i).start()

    own = [pltpu.make_async_copy(ins[a].at[me], outs[a].at[me], own_sem.at[a]) for a in range(3)]
    for copy in own:
        copy.start()
    for a in range(2):
        forward(a, ins[a].at[me], me)

    @pl.loop(1, seq)
    def _(i):
        src = lax.rem(me + seq - i, seq)
        for a in range(2):
            arrival(a, src).wait_recv()
            forward(a, outs[a].at[src], src)
        send(2, i).start()

    @pl.loop(1, seq)
    def _(i):
        src = lax.rem(me + seq - i, seq)
        arrival(2, src).wait_recv()
        for a in range(3):
            send(a, i).wait_send()

    for copy in own:
        copy.wait()

    @pl.when(has_high)
    def _():
        @pl.loop(0, seq)
        def _(src):
            for a in range(2):
                go_up(a, outs[a].at[src], src).wait_send()
                go_down(a, outs[a].at[src], src).wait_recv()

    @pl.when(has_low)
    def _():
        @pl.loop(0, seq)
        def _(src):
            for a in range(2):
                go_down(a, outs[a].at[src], src).wait_send()
                go_up(a, outs[a].at[src], src).wait_recv()


def attend_kernel(
    lengths_ref, q_ref, kl_ref, ko_ref, kh_ref, vl_ref, vo_ref, vh_ref, o_ref, *, bq, bk
):
    pack, cols = q_ref.shape
    heads = cols // HEAD
    tiles = pack // bk
    pack_base = lax.axis_index("dp") * pack
    base = pack_base - pack

    @pl.loop(0, pack // bq)
    def _(qt):
        r0 = pl.multiple_of(qt * bq, bq)
        first = pack_base + r0
        c_lo, s_lo, c_hi, e_hi = clip_range(lengths_ref, first, first + bq - 1)
        token = first + lax.broadcasted_iota(jnp.int32, (bq, HEAD), 0)

        def pick(c, carry):
            cum, start, end = carry
            inside = token >= cum
            nxt = cum + lengths_ref[c]
            return (nxt, jnp.where(inside, cum, start), jnp.where(inside, nxt, end))

        zeros = jnp.zeros((bq, HEAD), jnp.int32)
        _, start, end = lax.fori_loop(c_lo, c_hi + 1, pick, (s_lo, zeros, zeros))
        start = start[:, :1] - base
        end = end[:, :1] - base
        low = (s_lo - base) // bk
        high = (e_hi - base + bk - 1) // bk
        qs = [q_ref[pl.ds(r0, bq), h * HEAD : (h + 1) * HEAD] for h in range(heads)]

        def segment(k_ref, v_ref, seg, carry):
            def visit(t, carry):
                k0 = pl.multiple_of((t - seg * tiles) * bk, bk)
                idx = t * bk + lax.broadcasted_iota(jnp.int32, (bq, bk), 1)
                same = (idx >= start) & (idx < end)
                out = []
                for h in range(heads):
                    m, l, acc = carry[h]
                    hs = slice(h * HEAD, (h + 1) * HEAD)
                    k = k_ref[pl.ds(k0, bk), hs]
                    v = v_ref[pl.ds(k0, bk), hs]
                    s = lax.dot_general(
                        qs[h], k, (((1,), (1,)), ((), ())), preferred_element_type=jnp.float32
                    ) * SCORE_SCALE
                    s = jnp.where(same, s, MASK_FLOOR)
                    new_m = jnp.maximum(m, jnp.max(s, axis=1, keepdims=True))
                    w = jnp.exp(s - new_m)
                    shrink = jnp.exp(m - new_m)
                    l = l * shrink + jnp.sum(w, axis=1, keepdims=True)
                    acc = acc * shrink + jnp.dot(
                        w.astype(jnp.bfloat16), v, preferred_element_type=jnp.float32
                    )
                    out.append((new_m, l, acc))
                return tuple(out)

            return lax.fori_loop(
                jnp.maximum(low, seg * tiles), jnp.minimum(high, (seg + 1) * tiles), visit, carry
            )

        carry = tuple(
            (
                jnp.full((bq, 1), MASK_FLOOR, jnp.float32),
                jnp.zeros((bq, 1), jnp.float32),
                jnp.zeros((bq, HEAD), jnp.float32),
            )
            for _ in range(heads)
        )
        carry = segment(kl_ref, vl_ref, 0, carry)
        carry = segment(ko_ref, vo_ref, 1, carry)
        carry = segment(kh_ref, vh_ref, 2, carry)
        for h in range(heads):
            _, l, acc = carry[h]
            o_ref[pl.ds(r0, bq), h * HEAD : (h + 1) * HEAD] = (acc / l).astype(jnp.bfloat16)


def in_vmem():
    return pl.BlockSpec(memory_space=pltpu.VMEM)


def in_smem():
    return pl.BlockSpec(memory_space=pltpu.SMEM)


def shards(raw_query, raw_key, raw_value, query_gain, key_gain, lengths, clip_grids):
    _, rows, width = raw_query.shape
    seq = lax.axis_size("seq")
    pack = rows * seq
    cols = width // seq
    bk = math.gcd(pack, 512)
    bq = math.gcd(pack, 256)
    gains = jnp.stack([query_gain, swap_abs(query_gain), key_gain, swap_abs(key_gain)] * 2)
    part = jax.ShapeDtypeStruct((seq, rows, cols), jnp.bfloat16)
    q, k, v = pl.pallas_call(
        prep_kernel,
        out_shape=(part, part, part),
        in_specs=[in_smem(), in_smem()] + [in_vmem()] * 6,
        out_specs=(in_vmem(),) * 3,
        compiler_params=pltpu.CompilerParams(vmem_limit_bytes=VMEM_LIMIT),
        name="prep",
    )(
        lengths, clip_grids, raw_query[0], raw_key[0], raw_value[0],
        gains, angle_rates(), swap_matrix(),
    )

    def swap_all(x):
        return lax.all_to_all(x, "seq", split_axis=0, concat_axis=0, tiled=True)

    moved = pl.pallas_call(
        exchange_kernel,
        out_shape=(part,) * 7,
        in_specs=[pl.BlockSpec(memory_space=pl.ANY)] * 3,
        out_specs=(pl.BlockSpec(memory_space=pl.ANY),) * 7,
        scratch_shapes=[
            pltpu.SemaphoreType.DMA((3,)),
            pltpu.SemaphoreType.DMA((3, seq)),
            pltpu.SemaphoreType.DMA((3, seq)),
        ]
        + [pltpu.SemaphoreType.DMA((2, seq))] * 4,
        compiler_params=pltpu.CompilerParams(collective_id=0, has_side_effects=True),
        name="exchange",
    )(q, k, v)
    q, k, v, k_low, v_low, k_high, v_high = [x.reshape(pack, cols) for x in moved]
    out = pl.pallas_call(
        functools.partial(attend_kernel, bq=bq, bk=bk),
        out_shape=jax.ShapeDtypeStruct((pack, cols), jnp.bfloat16),
        in_specs=[in_smem()] + [in_vmem()] * 7,
        out_specs=in_vmem(),
        compiler_params=pltpu.CompilerParams(vmem_limit_bytes=VMEM_LIMIT),
        name="attend",
    )(lengths, q, k_low, k, k_high, v_low, v, v_high)
    out = swap_all(out.reshape(seq, rows, cols))
    return out.transpose(1, 0, 2).reshape(1, rows, width)


def solution(mesh):
    rows = P("dp", "seq", None)
    return jax.shard_map(
        shards,
        mesh=mesh,
        in_specs=(rows, rows, rows, P(), P(), P(), P()),
        out_specs=rows,
        check_vma=False,
    )
```

```python
import functools
import math

import jax
import jax.numpy as jnp
import numpy as np
from jax import lax
from jax.experimental import pallas as pl
from jax.experimental.pallas import tpu as pltpu
from jax.sharding import PartitionSpec as P

NORM_EPS = 1e-06
ROPE_THETA = 256.0
SCORE_SCALE = 1.0 / math.sqrt(128.0)
MASK_FLOOR = -1e30
HEAD = 128
VMEM_LIMIT = 62 * 1024 * 1024


def angle_rates():
    pair = np.arange(HEAD) // 2
    rates = np.zeros((8, HEAD), np.float64)
    rates[0] = np.where(pair < 8, ROPE_THETA ** (-2.0 * pair / 16.0), 0.0)
    rates[1] = np.where((pair >= 8) & (pair < 36), ROPE_THETA ** (-2.0 * (pair - 8.0) / 56.0), 0.0)
    rates[2] = np.where(pair >= 36, ROPE_THETA ** (-2.0 * (pair - 36.0) / 56.0), 0.0)
    return jnp.asarray(rates, jnp.float32)


def swap_matrix():
    m = np.zeros((HEAD, HEAD), np.float32)
    for k in range(HEAD // 2):
        m[2 * k + 1, 2 * k] = -1.0
        m[2 * k, 2 * k + 1] = 1.0
    return jnp.asarray(m, jnp.bfloat16)


def swap_abs(gain):
    return gain.reshape(-1, 2)[:, ::-1].reshape(-1)


def clip_range(lengths_ref, first_row, last_row):
    def step(c, carry):
        cum, c_lo, s_lo, c_hi, e_hi = carry
        end = cum + lengths_ref[c]
        in_lo = (first_row >= cum) & (first_row < end)
        in_hi = (last_row >= cum) & (last_row < end)
        return (
            end,
            jnp.where(in_lo, c, c_lo),
            jnp.where(in_lo, cum, s_lo),
            jnp.where(in_hi, c, c_hi),
            jnp.where(in_hi, end, e_hi),
        )

    zero = jnp.int32(0)
    out = lax.fori_loop(0, lengths_ref.shape[0], step, (zero, zero, zero, zero, zero))
    return out[1:]


def prep_kernel(
    lengths_ref, grids_ref, q_ref, k_ref, v_ref, gains_ref, rates_ref, swap_ref,
    qo_ref, ko_ref, vo_ref,
):
    rows, width = q_ref.shape
    parts, _, cols = qo_ref.shape
    seq_count = lax.axis_size("seq")
    first = (lax.axis_index("dp") * seq_count + lax.axis_index("seq")) * rows
    c_lo, s_lo, c_hi, _ = clip_range(lengths_ref, first, first + rows - 1)
    token = first + lax.broadcasted_iota(jnp.int32, (rows, HEAD), 0)

    def pick(c, carry):
        cum, start, high, wide = carry
        inside = token >= cum
        start = jnp.where(inside, cum, start)
        high = jnp.where(inside, grids_ref[c, 0].astype(jnp.float32), high)
        wide = jnp.where(inside, grids_ref[c, 1].astype(jnp.float32), wide)
        return (cum + lengths_ref[c], start, high, wide)

    ones = jnp.ones((rows, HEAD), jnp.float32)
    _, start, high, wide = lax.fori_loop(
        c_lo, c_hi + 1, pick, (s_lo, jnp.zeros((rows, HEAD), jnp.int32), ones, ones)
    )
    offset = (token - start).astype(jnp.float32)
    line = jnp.floor((offset + 0.5) / wide)
    col = offset - line * wide
    frame = jnp.floor((line + 0.5) / high)
    row = line - frame * high
    angles = frame * rates_ref[0:1] + row * rates_ref[1:2] + col * rates_ref[2:3]
    cosine = jnp.cos(angles)
    sine = jnp.sin(angles)
    swap = swap_ref[...]
    for x_ref, o_ref, g in ((k_ref, ko_ref, 2), (q_ref, qo_ref, 0)):
        cos_g = cosine
        gain, gain_sw = gains_ref[g : g + 1], gains_ref[g + 1 : g + 2]
        for h in range(width // HEAD):
            raw = x_ref[:, h * HEAD : (h + 1) * HEAD]
            x = raw.astype(jnp.float32)
            sw = jnp.dot(raw, swap, preferred_element_type=jnp.float32)
            inv = lax.rsqrt(jnp.mean(x * x, axis=-1, keepdims=True) + NORM_EPS)
            out = (x * inv * gain) * cos_g + (sw * inv * gain_sw) * sine
            p, o = (h * HEAD) // cols, (h * HEAD) % cols
            o_ref[p, :, o : o + HEAD] = out.astype(jnp.bfloat16)
    for p in range(parts):
        vo_ref[p] = v_ref[:, p * cols : (p + 1) * cols]


def remote(src, dst, send_sem, recv_sem, where):
    return pltpu.make_async_remote_copy(
        src_ref=src, dst_ref=dst, send_sem=send_sem, recv_sem=recv_sem,
        device_id=where, device_id_type=pl.DeviceIdType.MESH,
    )


def exchange_kernel(
    q_in, k_in, v_in, q_out, k_out, v_out, k_low, v_low, k_high, v_high,
    own_sem, send_sem, recv_sem, up_send, up_recv, down_send, down_recv,
):
    seq = lax.axis_size("seq")
    dp = lax.axis_size("dp")
    me = lax.axis_index("seq")
    pack = lax.axis_index("dp")
    has_low = pack > 0
    has_high = pack < dp - 1
    barrier = pltpu.get_barrier_semaphore()

    def signal(where):
        pl.semaphore_signal(barrier, inc=1, device_id=where, device_id_type=pl.DeviceIdType.MESH)

    @pl.loop(1, seq)
    def _(i):
        signal({"seq": lax.rem(me + i, seq)})

    signal({"dp": lax.rem(pack + 1, dp)})
    signal({"dp": lax.rem(pack + dp - 1, dp)})
    pl.semaphore_wait(barrier, seq + 1)

    ins = (k_in, v_in, q_in)
    outs = (k_out, v_out, q_out)
    lows = (k_low, v_low)
    highs = (k_high, v_high)

    def send(a, i):
        to = lax.rem(me + i, seq)
        return remote(
            ins[a].at[to], outs[a].at[me], send_sem.at[a, to], recv_sem.at[a, me], {"seq": to}
        )

    def arrival(a, src):
        return remote(
            ins[a].at[src], outs[a].at[src], send_sem.at[a, src], recv_sem.at[a, src],
            {"seq": src},
        )

    def go_up(a, src_ref, src):
        return remote(
            src_ref, lows[a].at[src], up_send.at[a, src], up_recv.at[a, src], {"dp": pack + 1}
        )

    def go_down(a, src_ref, src):
        return remote(
            src_ref, highs[a].at[src], down_send.at[a, src], down_recv.at[a, src],
            {"dp": pack - 1},
        )

    def forward(a, src_ref, src):
        @pl.when(has_high)
        def _():
            go_up(a, src_ref, src).start()

        @pl.when(has_low)
        def _():
            go_down(a, src_ref, src).start()

    @pl.loop(1, seq)
    def _(i):
        send(0, i).start()
        send(1, i).start()

    own = [pltpu.make_async_copy(ins[a].at[me], outs[a].at[me], own_sem.at[a]) for a in range(3)]
    for copy in own:
        copy.start()
    for a in range(2):
        forward(a, ins[a].at[me], me)

    @pl.loop(1, seq)
    def _(i):
        src = lax.rem(me + seq - i, seq)
        for a in range(2):
            arrival(a, src).wait_recv()
            forward(a, outs[a].at[src], src)
        send(2, i).start()

    @pl.loop(1, seq)
    def _(i):
        src = lax.rem(me + seq - i, seq)
        arrival(2, src).wait_recv()
        for a in range(3):
            send(a, i).wait_send()

    for copy in own:
        copy.wait()

    @pl.when(has_high)
    def _():
        @pl.loop(0, seq)
        def _(src):
            for a in range(2):
                go_up(a, outs[a].at[src], src).wait_send()
                go_down(a, outs[a].at[src], src).wait_recv()

    @pl.when(has_low)
    def _():
        @pl.loop(0, seq)
        def _(src):
            for a in range(2):
                go_down(a, outs[a].at[src], src).wait_send()
                go_up(a, outs[a].at[src], src).wait_recv()


def attend_kernel(
    lengths_ref, q_hbm, kl, ko, kh, vl, vo, vh, o_ref, q_ref, k_ref, v_ref, sems, *, head, bq, bk, chains
):
    pack = q_ref.shape[0]
    pack_base = lax.axis_index("dp") * pack
    base = pack_base - pack
    hs = pl.ds(head * HEAD, HEAD)
    copies = [pltpu.make_async_copy(q_hbm.at[:, hs], q_ref, sems.at[0])]
    for n, (src, dst) in enumerate(
        ((ko, k_ref), (vo, v_ref), (kl, k_ref), (vl, v_ref), (kh, k_ref), (vh, v_ref))
    ):
        place = (1, 0, 2)[n // 2] * pack
        copies.append(
            pltpu.make_async_copy(src.at[:, hs], dst.at[pl.ds(place, pack)], sems.at[n + 1])
        )
    for copy in copies:
        copy.start()
    for copy in copies:
        copy.wait()

    @pl.loop(0, pack // (bq * chains))
    def _(qt):
        r0 = pl.multiple_of(qt * (bq * chains), bq * chains)
        first = pack_base + r0
        c_lo, s_lo, c_hi, e_hi = clip_range(lengths_ref, first, first + bq * chains - 1)
        token = first + lax.broadcasted_iota(jnp.int32, (bq * chains, 1), 0)

        def pick(c, carry):
            cum, start, end = carry
            inside = token >= cum
            nxt = cum + lengths_ref[c]
            return (nxt, jnp.where(inside, cum, start), jnp.where(inside, nxt, end))

        zeros = jnp.zeros((bq * chains, 1), jnp.int32)
        _, start, end = lax.fori_loop(c_lo, c_hi + 1, pick, (s_lo, zeros, zeros))
        start = start - base
        end = end - base
        low = (s_lo - base) // bk
        high = (e_hi - base + bk - 1) // bk

        def visit(t, carry):
            k0 = pl.multiple_of(t * bk, bk)
            idx = k0 + lax.broadcasted_iota(jnp.int32, (bq, bk), 1)
            k = k_ref[pl.ds(k0, bk), :]
            v = v_ref[pl.ds(k0, bk), :]
            out = []
            for j in range(chains):
                m, l, acc = carry[j]
                rows = slice(j * bq, (j + 1) * bq)
                q = q_ref[pl.ds(r0 + j * bq, bq), :]
                s = lax.dot_general(
                    q, k, (((1,), (1,)), ((), ())), preferred_element_type=jnp.float32
                ) * SCORE_SCALE
                same = (idx >= start[rows]) & (idx < end[rows])
                s = jnp.where(same, s, MASK_FLOOR)
                new_m = jnp.maximum(m, jnp.max(s, axis=1, keepdims=True))
                w = jnp.exp(s - new_m)
                shrink = jnp.exp(m - new_m)
                l = l * shrink + jnp.sum(w, axis=1, keepdims=True)
                acc = acc * shrink + jnp.dot(
                    w.astype(jnp.bfloat16), v, preferred_element_type=jnp.float32
                )
                out.append((new_m, l, acc))
            return tuple(out)

        carry = tuple(
            (
                jnp.full((bq, 1), MASK_FLOOR, jnp.float32),
                jnp.zeros((bq, 1), jnp.float32),
                jnp.zeros((bq, HEAD), jnp.float32),
            )
            for _ in range(chains)
        )
        carry = lax.fori_loop(low, high, visit, carry)
        for j in range(chains):
            _, l, acc = carry[j]
            o_ref[pl.ds(r0 + j * bq, bq), :] = (acc / l).astype(jnp.bfloat16)


def in_vmem():
    return pl.BlockSpec(memory_space=pltpu.VMEM)


def in_smem():
    return pl.BlockSpec(memory_space=pltpu.SMEM)


def shards(raw_query, raw_key, raw_value, query_gain, key_gain, lengths, clip_grids):
    _, rows, width = raw_query.shape
    seq = lax.axis_size("seq")
    pack = rows * seq
    cols = width // seq
    bk = math.gcd(pack, 512)
    bq = math.gcd(pack, 256)
    gains = jnp.stack([query_gain, swap_abs(query_gain), key_gain, swap_abs(key_gain)] * 2)
    part = jax.ShapeDtypeStruct((seq, rows, cols), jnp.bfloat16)
    q, k, v = pl.pallas_call(
        prep_kernel,
        out_shape=(part, part, part),
        in_specs=[in_smem(), in_smem()] + [in_vmem()] * 6,
        out_specs=(in_vmem(),) * 3,
        compiler_params=pltpu.CompilerParams(vmem_limit_bytes=VMEM_LIMIT),
        name="prep",
    )(
        lengths, clip_grids, raw_query[0], raw_key[0], raw_value[0],
        gains, angle_rates(), swap_matrix(),
    )

    def swap_all(x):
        return lax.all_to_all(x, "seq", split_axis=0, concat_axis=0, tiled=True)

    moved = pl.pallas_call(
        exchange_kernel,
        out_shape=(part,) * 7,
        in_specs=[pl.BlockSpec(memory_space=pl.ANY)] * 3,
        out_specs=(pl.BlockSpec(memory_space=pl.ANY),) * 7,
        scratch_shapes=[
            pltpu.SemaphoreType.DMA((3,)),
            pltpu.SemaphoreType.DMA((3, seq)),
            pltpu.SemaphoreType.DMA((3, seq)),
        ]
        + [pltpu.SemaphoreType.DMA((2, seq))] * 4,
        compiler_params=pltpu.CompilerParams(collective_id=0, has_side_effects=True),
        name="exchange",
    )(q, k, v)
    q, k, v, k_low, v_low, k_high, v_high = [x.reshape(pack, cols) for x in moved]
    results = []
    for head in range(cols // HEAD):
        out = pl.pallas_call(
            functools.partial(attend_kernel, head=head, bq=bq, bk=bk, chains=bk // bq),
            out_shape=jax.ShapeDtypeStruct((pack, HEAD), jnp.bfloat16),
            in_specs=[in_smem()] + [pl.BlockSpec(memory_space=pl.ANY)] * 7,
            out_specs=in_vmem(),
            scratch_shapes=[
                pltpu.VMEM((pack, HEAD), jnp.bfloat16),
                pltpu.VMEM((3 * pack, HEAD), jnp.bfloat16),
                pltpu.VMEM((3 * pack, HEAD), jnp.bfloat16),
                pltpu.SemaphoreType.DMA((7,)),
            ],
            compiler_params=pltpu.CompilerParams(vmem_limit_bytes=VMEM_LIMIT),
            cost_estimate=pl.CostEstimate(
                flops=8 * pack * pack * HEAD,
                bytes_accessed=16 * pack * HEAD,
                transcendentals=pack * pack,
            ),
            name="attend",
        )(lengths, q, k_low, k, k_high, v_low, v, v_high)
        results.append(swap_all(out.reshape(seq, rows, HEAD)))
    out = jnp.concatenate(results, axis=2)
    return out.transpose(1, 0, 2).reshape(1, rows, width)


def solution(mesh):
    rows = P("dp", "seq", None)
    return jax.shard_map(
        shards,
        mesh=mesh,
        in_specs=(rows, rows, rows, P(), P(), P(), P()),
        out_specs=rows,
        check_vma=False,
    )
```

```python
import functools
import math

import jax
import jax.numpy as jnp
import numpy as np
from jax import lax
from jax.experimental import pallas as pl
from jax.experimental.pallas import tpu as pltpu
from jax.sharding import PartitionSpec as P

NORM_EPS = 1e-06
ROPE_THETA = 256.0
SCORE_SCALE = 1.0 / math.sqrt(128.0)
MASK_FLOOR = -1e30
HEAD = 128
VMEM_LIMIT = 62 * 1024 * 1024


def angle_rates():
    pair = np.arange(HEAD) // 2
    rates = np.zeros((8, HEAD), np.float64)
    rates[0] = np.where(pair < 8, ROPE_THETA ** (-2.0 * pair / 16.0), 0.0)
    rates[1] = np.where((pair >= 8) & (pair < 36), ROPE_THETA ** (-2.0 * (pair - 8.0) / 56.0), 0.0)
    rates[2] = np.where(pair >= 36, ROPE_THETA ** (-2.0 * (pair - 36.0) / 56.0), 0.0)
    return jnp.asarray(rates, jnp.float32)


def swap_matrix():
    m = np.zeros((HEAD, HEAD), np.float32)
    for k in range(HEAD // 2):
        m[2 * k + 1, 2 * k] = -1.0
        m[2 * k, 2 * k + 1] = 1.0
    return jnp.asarray(m, jnp.bfloat16)


def swap_abs(gain):
    return gain.reshape(-1, 2)[:, ::-1].reshape(-1)


def clip_range(lengths_ref, first_row, last_row):
    def step(c, carry):
        cum, c_lo, s_lo, c_hi, e_hi = carry
        end = cum + lengths_ref[c]
        in_lo = (first_row >= cum) & (first_row < end)
        in_hi = (last_row >= cum) & (last_row < end)
        return (
            end,
            jnp.where(in_lo, c, c_lo),
            jnp.where(in_lo, cum, s_lo),
            jnp.where(in_hi, c, c_hi),
            jnp.where(in_hi, end, e_hi),
        )

    zero = jnp.int32(0)
    out = lax.fori_loop(0, lengths_ref.shape[0], step, (zero, zero, zero, zero, zero))
    return out[1:]


def prep_kernel(
    lengths_ref, grids_ref, q_ref, k_ref, v_ref, gains_ref, rates_ref, swap_ref,
    qo_ref, ko_ref, vo_ref,
):
    rows, width = q_ref.shape
    parts, _, cols = qo_ref.shape
    seq_count = lax.axis_size("seq")
    first = (lax.axis_index("dp") * seq_count + lax.axis_index("seq")) * rows
    c_lo, s_lo, c_hi, _ = clip_range(lengths_ref, first, first + rows - 1)
    token = first + lax.broadcasted_iota(jnp.int32, (rows, HEAD), 0)

    def pick(c, carry):
        cum, start, high, wide = carry
        inside = token >= cum
        start = jnp.where(inside, cum, start)
        high = jnp.where(inside, grids_ref[c, 0].astype(jnp.float32), high)
        wide = jnp.where(inside, grids_ref[c, 1].astype(jnp.float32), wide)
        return (cum + lengths_ref[c], start, high, wide)

    ones = jnp.ones((rows, HEAD), jnp.float32)
    _, start, high, wide = lax.fori_loop(
        c_lo, c_hi + 1, pick, (s_lo, jnp.zeros((rows, HEAD), jnp.int32), ones, ones)
    )
    offset = (token - start).astype(jnp.float32)
    line = jnp.floor((offset + 0.5) / wide)
    col = offset - line * wide
    frame = jnp.floor((line + 0.5) / high)
    row = line - frame * high
    angles = frame * rates_ref[0:1] + row * rates_ref[1:2] + col * rates_ref[2:3]
    cosine = jnp.cos(angles)
    sine = jnp.sin(angles)
    swap = swap_ref[...]
    for x_ref, o_ref, g in ((k_ref, ko_ref, 2), (q_ref, qo_ref, 0)):
        cos_g = cosine
        gain, gain_sw = gains_ref[g : g + 1], gains_ref[g + 1 : g + 2]
        for h in range(width // HEAD):
            raw = x_ref[:, h * HEAD : (h + 1) * HEAD]
            x = raw.astype(jnp.float32)
            sw = jnp.dot(raw, swap, preferred_element_type=jnp.float32)
            inv = lax.rsqrt(jnp.mean(x * x, axis=-1, keepdims=True) + NORM_EPS)
            out = (x * inv * gain) * cos_g + (sw * inv * gain_sw) * sine
            p, o = (h * HEAD) // cols, (h * HEAD) % cols
            o_ref[p, :, o : o + HEAD] = out.astype(jnp.bfloat16)
    for p in range(parts):
        vo_ref[p] = v_ref[:, p * cols : (p + 1) * cols]


def remote(src, dst, send_sem, recv_sem, where):
    return pltpu.make_async_remote_copy(
        src_ref=src, dst_ref=dst, send_sem=send_sem, recv_sem=recv_sem,
        device_id=where, device_id_type=pl.DeviceIdType.MESH,
    )


def exchange_kernel(
    q_in, k_in, v_in, q_out, k_out, v_out, k_low, v_low, k_high, v_high,
    own_sem, send_sem, recv_sem, up_send, up_recv, down_send, down_recv,
):
    seq = lax.axis_size("seq")
    dp = lax.axis_size("dp")
    me = lax.axis_index("seq")
    pack = lax.axis_index("dp")
    has_low = pack > 0
    has_high = pack < dp - 1
    barrier = pltpu.get_barrier_semaphore()

    def signal(where):
        pl.semaphore_signal(barrier, inc=1, device_id=where, device_id_type=pl.DeviceIdType.MESH)

    @pl.loop(1, seq)
    def _(i):
        signal({"seq": lax.rem(me + i, seq)})

    signal({"dp": lax.rem(pack + 1, dp)})
    signal({"dp": lax.rem(pack + dp - 1, dp)})
    pl.semaphore_wait(barrier, seq + 1)

    ins = (k_in, v_in, q_in)
    outs = (k_out, v_out, q_out)
    lows = (k_low, v_low)
    highs = (k_high, v_high)

    def send(a, i):
        to = lax.rem(me + i, seq)
        return remote(
            ins[a].at[to], outs[a].at[me], send_sem.at[a, to], recv_sem.at[a, me], {"seq": to}
        )

    def arrival(a, src):
        return remote(
            ins[a].at[src], outs[a].at[src], send_sem.at[a, src], recv_sem.at[a, src],
            {"seq": src},
        )

    def go_up(a, src_ref, src):
        return remote(
            src_ref, lows[a].at[src], up_send.at[a, src], up_recv.at[a, src], {"dp": pack + 1}
        )

    def go_down(a, src_ref, src):
        return remote(
            src_ref, highs[a].at[src], down_send.at[a, src], down_recv.at[a, src],
            {"dp": pack - 1},
        )

    def forward(a, src_ref, src):
        @pl.when(has_high)
        def _():
            go_up(a, src_ref, src).start()

        @pl.when(has_low)
        def _():
            go_down(a, src_ref, src).start()

    @pl.loop(1, seq)
    def _(i):
        send(0, i).start()
        send(1, i).start()

    own = [pltpu.make_async_copy(ins[a].at[me], outs[a].at[me], own_sem.at[a]) for a in range(3)]
    for copy in own:
        copy.start()
    for a in range(2):
        forward(a, ins[a].at[me], me)

    @pl.loop(1, seq)
    def _(i):
        src = lax.rem(me + seq - i, seq)
        for a in range(2):
            arrival(a, src).wait_recv()
            forward(a, outs[a].at[src], src)
        send(2, i).start()

    @pl.loop(1, seq)
    def _(i):
        src = lax.rem(me + seq - i, seq)
        arrival(2, src).wait_recv()
        for a in range(3):
            send(a, i).wait_send()

    for copy in own:
        copy.wait()

    @pl.when(has_high)
    def _():
        @pl.loop(0, seq)
        def _(src):
            for a in range(2):
                go_up(a, outs[a].at[src], src).wait_send()
                go_down(a, outs[a].at[src], src).wait_recv()

    @pl.when(has_low)
    def _():
        @pl.loop(0, seq)
        def _(src):
            for a in range(2):
                go_down(a, outs[a].at[src], src).wait_send()
                go_up(a, outs[a].at[src], src).wait_recv()


def attend_kernel(
    lengths_ref, q_hbm, kl, ko, kh, vl, vo, vh, o_ref, q_ref, k_ref, v_ref, sems, *, head, bq, bk, chains
):
    pack = q_ref.shape[0]
    pack_base = lax.axis_index("dp") * pack
    base = pack_base - pack
    hs = pl.ds(head * HEAD, HEAD)
    copies = [pltpu.make_async_copy(q_hbm.at[:, hs], q_ref, sems.at[0])]
    for n, (src, dst) in enumerate(
        ((ko, k_ref), (vo, v_ref), (kl, k_ref), (vl, v_ref), (kh, k_ref), (vh, v_ref))
    ):
        place = (1, 0, 2)[n // 2] * pack
        copies.append(
            pltpu.make_async_copy(src.at[:, hs], dst.at[pl.ds(place, pack)], sems.at[n + 1])
        )
    for copy in copies:
        copy.start()
    for copy in copies:
        copy.wait()

    @pl.loop(0, pack // (bq * chains))
    def _(qt):
        r0 = pl.multiple_of(qt * (bq * chains), bq * chains)
        first = pack_base + r0
        c_lo, s_lo, c_hi, e_hi = clip_range(lengths_ref, first, first + bq * chains - 1)
        token = first + lax.broadcasted_iota(jnp.int32, (bq * chains, 1), 0)

        def pick(c, carry):
            cum, start, end = carry
            inside = token >= cum
            nxt = cum + lengths_ref[c]
            return (nxt, jnp.where(inside, cum, start), jnp.where(inside, nxt, end))

        zeros = jnp.zeros((bq * chains, 1), jnp.int32)
        _, start, end = lax.fori_loop(c_lo, c_hi + 1, pick, (s_lo, zeros, zeros))
        start = start - base
        end = end - base
        low = (s_lo - base) // bk
        high = (e_hi - base + bk - 1) // bk

        def visit(masked, t, carry):
            k0 = pl.multiple_of(t * bk, bk)
            idx = k0 + lax.broadcasted_iota(jnp.int32, (bq, bk), 1)
            k = k_ref[pl.ds(k0, bk), :]
            v = v_ref[pl.ds(k0, bk), :]
            out = []
            for j in range(chains):
                m, l, acc = carry[j]
                rows = slice(j * bq, (j + 1) * bq)
                q = q_ref[pl.ds(r0 + j * bq, bq), :]
                s = lax.dot_general(
                    q, k, (((1,), (1,)), ((), ())), preferred_element_type=jnp.float32
                ) * SCORE_SCALE
                if masked:
                    same = (idx >= start[rows]) & (idx < end[rows])
                    s = jnp.where(same, s, MASK_FLOOR)
                new_m = jnp.maximum(m, jnp.max(s, axis=1, keepdims=True))
                w = jnp.exp(s - new_m)
                shrink = jnp.exp(m - new_m)
                l = l * shrink + jnp.sum(w, axis=1, keepdims=True)
                acc = acc * shrink + jnp.dot(
                    w.astype(jnp.bfloat16), v, preferred_element_type=jnp.float32
                )
                out.append((new_m, l, acc))
            return tuple(out)

        carry = tuple(
            (
                jnp.full((bq, 1), MASK_FLOOR, jnp.float32),
                jnp.zeros((bq, 1), jnp.float32),
                jnp.zeros((bq, HEAD), jnp.float32),
            )
            for _ in range(chains)
        )
        whole_low = jnp.where(c_lo == c_hi, (s_lo - base + bk - 1) // bk, high)
        whole_high = jnp.where(c_lo == c_hi, (e_hi - base) // bk, high)
        whole_low = jnp.minimum(whole_low, high)
        whole_high = jnp.maximum(whole_high, whole_low)
        edge, whole = functools.partial(visit, True), functools.partial(visit, False)
        carry = lax.fori_loop(low, whole_low, edge, carry)
        carry = lax.fori_loop(whole_low, whole_high, whole, carry)
        carry = lax.fori_loop(whole_high, high, edge, carry)
        for j in range(chains):
            _, l, acc = carry[j]
            o_ref[pl.ds(r0 + j * bq, bq), :] = (acc / l).astype(jnp.bfloat16)


def in_vmem():
    return pl.BlockSpec(memory_space=pltpu.VMEM)


def in_smem():
    return pl.BlockSpec(memory_space=pltpu.SMEM)


def shards(raw_query, raw_key, raw_value, query_gain, key_gain, lengths, clip_grids):
    _, rows, width = raw_query.shape
    seq = lax.axis_size("seq")
    pack = rows * seq
    cols = width // seq
    bk = math.gcd(pack, 512)
    bq = math.gcd(pack, 256)
    gains = jnp.stack([query_gain, swap_abs(query_gain), key_gain, swap_abs(key_gain)] * 2)
    part = jax.ShapeDtypeStruct((seq, rows, cols), jnp.bfloat16)
    q, k, v = pl.pallas_call(
        prep_kernel,
        out_shape=(part, part, part),
        in_specs=[in_smem(), in_smem()] + [in_vmem()] * 6,
        out_specs=(in_vmem(),) * 3,
        compiler_params=pltpu.CompilerParams(vmem_limit_bytes=VMEM_LIMIT),
        name="prep",
    )(
        lengths, clip_grids, raw_query[0], raw_key[0], raw_value[0],
        gains, angle_rates(), swap_matrix(),
    )

    def swap_all(x):
        return lax.all_to_all(x, "seq", split_axis=0, concat_axis=0, tiled=True)

    moved = pl.pallas_call(
        exchange_kernel,
        out_shape=(part,) * 7,
        in_specs=[pl.BlockSpec(memory_space=pl.ANY)] * 3,
        out_specs=(pl.BlockSpec(memory_space=pl.ANY),) * 7,
        scratch_shapes=[
            pltpu.SemaphoreType.DMA((3,)),
            pltpu.SemaphoreType.DMA((3, seq)),
            pltpu.SemaphoreType.DMA((3, seq)),
        ]
        + [pltpu.SemaphoreType.DMA((2, seq))] * 4,
        compiler_params=pltpu.CompilerParams(collective_id=0, has_side_effects=True),
        name="exchange",
    )(q, k, v)
    q, k, v, k_low, v_low, k_high, v_high = [x.reshape(pack, cols) for x in moved]
    results = []
    for head in range(cols // HEAD):
        out = pl.pallas_call(
            functools.partial(attend_kernel, head=head, bq=bq, bk=bk, chains=bk // bq),
            out_shape=jax.ShapeDtypeStruct((pack, HEAD), jnp.bfloat16),
            in_specs=[in_smem()] + [pl.BlockSpec(memory_space=pl.ANY)] * 7,
            out_specs=in_vmem(),
            scratch_shapes=[
                pltpu.VMEM((pack, HEAD), jnp.bfloat16),
                pltpu.VMEM((3 * pack, HEAD), jnp.bfloat16),
                pltpu.VMEM((3 * pack, HEAD), jnp.bfloat16),
                pltpu.SemaphoreType.DMA((7,)),
            ],
            compiler_params=pltpu.CompilerParams(vmem_limit_bytes=VMEM_LIMIT),
            cost_estimate=pl.CostEstimate(
                flops=8 * pack * pack * HEAD,
                bytes_accessed=16 * pack * HEAD,
                transcendentals=pack * pack,
            ),
            name="attend",
        )(lengths, q, k_low, k, k_high, v_low, v, v_high)
        results.append(swap_all(out.reshape(seq, rows, HEAD)))
    out = jnp.concatenate(results, axis=2)
    return out.transpose(1, 0, 2).reshape(1, rows, width)


def solution(mesh):
    rows = P("dp", "seq", None)
    return jax.shard_map(
        shards,
        mesh=mesh,
        in_specs=(rows, rows, rows, P(), P(), P(), P()),
        out_specs=rows,
        check_vma=False,
    )
```
